128 devices in a mesh: row: 16 (over x, z), col: 8 (over y, core).
Axes of the slice: x: 4, y: 4, z: 4, core: 2. Of those that a mesh axis runs over, the one named last changes fastest.
Arguments:
- excitation: bfloat16 [131072, 128], P(('row', 'col')), may hold values from -6 to 6
- near_list: int32 [1024, 5], P(('row', 'col')), may hold values from 0 to 1023, as said below
- near_blocks: bfloat16 [2, 131072, 640], P(None, ('row', 'col')), may hold values from -0.15625 to 0.15625
- col_factors: bfloat16 [2, 131072, 2048], P(None, ('row', 'col')), may hold values from -0.125 to 0.125
- coupling: bfloat16 [2, 131072, 2048], P(None, ('row', 'col')), may hold values from -0.09375 to 0.09375
- row_factors: bfloat16 [2, 131072, 1024], P(None, ('row', 'col')), may hold values from -0.125 to 0.125
Outputs:
- response: bfloat16 [131072, 128], P(('row', 'col'))
The draws below stay inside these ranges and needn't reach their ends.
Inputs may be any that keep to these rules, and one draw needn't show every extreme that they name: near_list[i, 0] = i; every entry lies within 8 leaves of i, and leaves at distance exactly 8 on either side occur.
All inputs are finite; a program needn't handle non-finite values.
Results may differ from the reference program's by a relative error of at most 0.008.
Values may be sent and summed in bfloat16 or wider, within the bound.
A program may use at most 128 MiB of HBM per device.

```python
import jax
import jax.numpy as jnp
from jax import lax

UNK_DEV = 1024
EXCITE = 64
RANK = 128
LEAF = 128
REACH = 8
NEAR = 5
COLS = 128
UNKNOWNS = 131072
LEAVES = 1024
ROW_RANKS = 2048
COL_RANKS = 1024
COUPLE_ROWS = 131072
N_ROW = 16
N_COL = 8


def draw_near_list(key, part):
    first_key, second_key = jax.random.split(jax.random.fold_in(key, 17))
    base = jnp.arange(LEAVES, dtype=jnp.int32)[:, None]
    offsets = jax.random.randint(first_key, (LEAVES, NEAR - 2), -REACH, REACH + 1, dtype=jnp.int32)
    direction = jax.random.randint(second_key, (LEAVES, 1), 0, 2, dtype=jnp.int32) * 2 - 1
    steps_all = jnp.concatenate([jnp.zeros((LEAVES, 1), jnp.int32), offsets, direction * REACH], axis=1)
    return jnp.clip(base + steps_all, 0, LEAVES - 1).astype(jnp.int32)


def block_levels(key, dims, shards, least, top_value):
    def one(position, shards_of):
        heights = jax.random.uniform(jax.random.fold_in(jax.random.fold_in(key, 6), position), (shards_of,), jnp.float32, least / len(shards), top_value / len(shards))
        return jnp.repeat(jnp.exp(heights), dims[position] // shards_of).reshape((-1,) + (1,) * (len(dims) - position - 1))

    level = one(*shards[0])
    for cut in shards[1:]:
        level = level * one(*cut)
    return level


def noise(key, shape, deviation, reach, shards=(), kind=jnp.bfloat16):
    gain = block_levels(key, shape, shards, -0.22, 0.18) if shards else 1.0
    result = jax.random.normal(key, shape, jnp.float32) * deviation * gain
    return jnp.minimum(jnp.maximum(result, -reach), reach).astype(kind)


def setup_inputs(seed: int = 0) -> dict:
    seeds = jax.random.split(jax.random.key(seed), 7)
    excitation = noise(seeds[0], (UNKNOWNS, COLS), 1.0, 6.0, ((0, 128),))
    near_list = draw_near_list(jax.random.fold_in(seeds[6], 71), 0)
    near_blocks = noise(seeds[2], (2, UNKNOWNS, NEAR * LEAF), (2 * NEAR * LEAF) ** -0.5, 0.15625, ((1, 128),))
    col_factors = noise(seeds[3], (2, UNKNOWNS, ROW_RANKS), (2 * UNK_DEV) ** -0.5, 0.125, ((1, 128),))
    coupling = noise(seeds[4], (2, COUPLE_ROWS, ROW_RANKS), (2 * ROW_RANKS) ** -0.5, 0.09375, ((1, 128),))
    row_factors = noise(seeds[5], (2, UNKNOWNS, COL_RANKS), (2 * COL_RANKS) ** -0.5, 0.125, ((1, 128),))
    return {"excitation": excitation, "near_list": near_list, "near_blocks": near_blocks, "col_factors": col_factors, "coupling": coupling, "row_factors": row_factors}


def rotate_parts(data, axis):
    real_side = lax.slice_in_dim(data, 0, 1, axis=axis)
    imag_side = lax.slice_in_dim(data, 1, 2, axis=axis)
    return jnp.concatenate([-imag_side, real_side], axis=axis)


def multiply(real_part, imag_part, data):
    count = data.shape[0]
    flattened = data.reshape(count, -1)
    turned = rotate_parts(data, 1).reshape(count, -1)
    summed = jnp.dot(real_part, flattened, preferred_element_type=jnp.float32)
    summed = summed + jnp.dot(imag_part, turned, preferred_element_type=jnp.float32)
    return summed.reshape(real_part.shape[0], 2, -1)


def project(real_part, imag_part, data):
    count = data.shape[0]
    flattened = data.reshape(count, -1)
    turned = rotate_parts(data, 1).reshape(count, -1)
    contract_dims = (((0,), (0,)), ((), ()))
    summed = lax.dot_general(real_part, flattened, contract_dims, preferred_element_type=jnp.float32)
    summed = summed + lax.dot_general(imag_part, turned, contract_dims, preferred_element_type=jnp.float32)
    return summed.reshape(real_part.shape[1], 2, -1)


def multiply_split(real_part, imag_part, data):
    upper_part = data.astype(jnp.bfloat16)
    lower_part = (data - upper_part.astype(jnp.float32)).astype(jnp.bfloat16)
    return multiply(real_part, imag_part, upper_part) + multiply(real_part, imag_part, lower_part)


def reference(excitation, near_list, near_blocks, col_factors, coupling, row_factors):
    clusters = N_ROW * N_COL
    leaves_x = excitation.reshape(LEAVES, LEAF, COLS)
    gathered = leaves_x[near_list].reshape(LEAVES, NEAR * LEAF, 2, EXCITE)
    turned = rotate_parts(gathered, 2).reshape(LEAVES, NEAR * LEAF, COLS)
    gathered = gathered.reshape(LEAVES, NEAR * LEAF, COLS)
    blocks_re = near_blocks[0].reshape(LEAVES, LEAF, NEAR * LEAF).astype(jnp.float32)
    blocks_im = near_blocks[1].reshape(LEAVES, LEAF, NEAR * LEAF).astype(jnp.float32)
    near_field = jnp.einsum("ilm,imc->ilc", blocks_re, gathered.astype(jnp.float32))
    near_field = near_field + jnp.einsum("ilm,imc->ilc", blocks_im, turned.astype(jnp.float32))
    near_field = near_field.reshape(UNKNOWNS, COLS)

    shaped = excitation.reshape(clusters, UNK_DEV, 2, EXCITE)
    vreal = col_factors[0].reshape(clusters, UNK_DEV, ROW_RANKS)
    vimag = col_factors[1].reshape(clusters, UNK_DEV, ROW_RANKS)
    compressed = lax.map(lambda operands: project(operands[0], operands[1], operands[2]), (vreal, vimag, shaped))
    compressed = compressed.reshape(N_ROW, N_COL, N_ROW, RANK, 2, EXCITE).transpose(2, 1, 0, 3, 4, 5)
    arrived = compressed.reshape(clusters, ROW_RANKS, 2, EXCITE)

    breal = coupling[0].reshape(clusters, COL_RANKS, ROW_RANKS)
    bimag = coupling[1].reshape(clusters, COL_RANKS, ROW_RANKS)
    middle = lax.map(lambda operands: multiply_split(operands[0], operands[1], operands[2]), (breal, bimag, arrived))
    middle = middle.reshape(N_ROW, N_COL, N_COL, RANK, 2, EXCITE).transpose(0, 2, 1, 3, 4, 5)
    landed = middle.reshape(clusters, COL_RANKS, 2, EXCITE)

    ureal = row_factors[0].reshape(clusters, UNK_DEV, COL_RANKS)
    uimag = row_factors[1].reshape(clusters, UNK_DEV, COL_RANKS)
    far_field = lax.map(lambda operands: multiply_split(operands[0], operands[1], operands[2]), (ureal, uimag, landed))
    far_field = far_field.reshape(UNKNOWNS, COLS)
    return (near_field + far_field).astype(jnp.bfloat16)
```

```python
import functools

import jax
import jax.numpy as jnp
from jax import lax
from jax.experimental import pallas as pl
from jax.experimental.pallas import tpu as pltpu
from jax.sharding import PartitionSpec as P

RANK = 128
LEAF = 128
NEAR = 5
MESH = pl.DeviceIdType.MESH
BF16 = jnp.bfloat16
F32 = jnp.float32


def ring_order(count):
    return sorted(range(count), key=lambda k: (-min(k, count - k), k))


def turn(data):
    half = data.shape[1] // 2
    wide = data.astype(F32)
    rolled = pltpu.roll(wide, half, 1)
    lane = lax.broadcasted_iota(jnp.int32, wide.shape, 1)
    return jnp.where(lane < half, -rolled, rolled).astype(BF16)


def dot(a, b):
    return jnp.dot(a, b, preferred_element_type=F32)


def kernel(
    nx, nz, ny, nc,
    x_hbm, list_ref, near_hbm, col_hbm, mid_hbm, row_hbm, out_ref,
    table, turned, near, col, mid, row, xt, csend, arrived, tz, acc, msend, landed, far,
    x_sem, near_sem, col_sem, mid_sem, row_sem,
    halo_send, halo_recv, a_send, a_recv, b_send, b_recv,
):
    leaves = x_hbm.shape[0]
    unk = leaves * LEAF
    my_row, my_col = lax.axis_index("row"), lax.axis_index("col")
    x, z = my_row // nz, my_row % nz
    y, core = my_col // nc, my_col % nc
    n_col, n_all = ny * nc, nx * nz * ny * nc
    x_offs, z_offs, y_offs, c_offs = (ring_order(n) for n in (nx, nz, ny, nc))
    wx, wy = nz * RANK, nc * RANK

    me = my_row * n_col + my_col
    after = (me + 1) % n_all
    before = (me + n_all - 1) % n_all
    after_id = (after // n_col, after % n_col)
    before_id = (before // n_col, before % n_col)

    own = table.at[pl.ds(leaves, leaves)]
    load_x = pltpu.make_async_copy(x_hbm, own, x_sem)
    load_x.start()

    def span(position, width):
        return pl.ds(pl.multiple_of(position * width, width), width)

    load_col = [
        pltpu.make_async_copy(col_hbm.at[:, :, span((x + off) % nx, wx)], col.at[s], col_sem.at[s])
        for s, off in enumerate(x_offs)
    ]
    load_mid = [
        pltpu.make_async_copy(mid_hbm.at[:, :, span((x + nx - off) % nx, wx)], mid.at[s], mid_sem.at[s])
        for s, off in enumerate(x_offs)
    ]
    load_row = [
        pltpu.make_async_copy(row_hbm.at[:, :, span((y + ny - off) % ny, wy)], row.at[t], row_sem.at[t])
        for t, off in enumerate(y_offs)
    ]
    load_near = pltpu.make_async_copy(near_hbm, near, near_sem)
    for copy in load_col:
        copy.start()

    barrier = pltpu.get_barrier_semaphore()
    greeted = 0
    for off_x in range(nx):
        for off_z in range(nz):
            if off_x or off_z:
                peer = ((x + off_x) % nx * nz + (z + off_z) % nz, my_col)
                pl.semaphore_signal(barrier, inc=1, device_id=peer, device_id_type=MESH)
                greeted += 1
    for off in range(1, n_col):
        pl.semaphore_signal(barrier, inc=1, device_id=(my_row, (my_col + off) % n_col), device_id_type=MESH)
        greeted += 1
    for peer in (after_id, before_id):
        pl.semaphore_signal(barrier, inc=1, device_id=peer, device_id_type=MESH)
        greeted += 1
    pl.semaphore_wait(barrier, greeted)

    halo = [
        pltpu.make_async_remote_copy(
            x_hbm, table.at[pl.ds(0, leaves)], halo_send.at[0], halo_recv.at[0],
            device_id=after_id, device_id_type=MESH,
        ),
        pltpu.make_async_remote_copy(
            x_hbm, table.at[pl.ds(2 * leaves, leaves)], halo_send.at[1], halo_recv.at[1],
            device_id=before_id, device_id_type=MESH,
        ),
    ]
    for copy in halo:
        copy.start()

    load_x.wait()
    mine = table[pl.ds(leaves, leaves)].reshape(unk, LEAF)
    flipped = mine.astype(F32).T.astype(BF16)
    half = flipped.shape[0] // 2
    xt[0] = flipped
    xt[1] = jnp.concatenate([-flipped[half:], flipped[:half]], axis=0)
    turned[pl.ds(leaves, leaves)] = turn(mine).reshape(leaves, LEAF, LEAF)

    later = [[load_near], load_mid[:1], load_mid[1:2], load_mid[2:]]
    a_copies = []
    for s, off_x in enumerate(x_offs):
        load_col[s].wait()
        for copy in later[s] if s < len(later) else ():
            copy.start()
        block = dot(xt[0], col[s, 0]) + dot(xt[1], col[s, 1])
        for j in range(nz):
            csend[s, j] = block[:, j * RANK : (j + 1) * RANK].T.astype(BF16)
        for off_z in z_offs:
            to_z = (z + off_z) % nz
            if off_x == 0 and off_z == 0:
                arrived[s, pl.ds(pl.multiple_of(z * RANK, RANK), RANK), :] = csend[s, z]
                continue
            copy = pltpu.make_async_remote_copy(
                csend.at[s, to_z],
                arrived.at[s, pl.ds(pl.multiple_of(z * RANK, RANK), RANK)],
                a_send.at[s, to_z],
                a_recv.at[s, z],
                device_id=((x + off_x) % nx * nz + to_z, my_col),
                device_id_type=MESH,
            )
            copy.start()
            a_copies.append(copy)
    for copies in later[len(x_offs) :]:
        for copy in copies:
            copy.start()
    for copy in load_row:
        copy.start()

    for copy in halo:
        copy.wait_recv()
    load_near.wait()
    for start in (0, 2 * leaves):
        side = table[pl.ds(start, leaves)].reshape(unk, LEAF)
        turned[pl.ds(start, leaves)] = turn(side).reshape(leaves, LEAF, LEAF)
    first = me * leaves - leaves
    for i in range(leaves):
        total = None
        rows = pl.ds(i * LEAF, LEAF)
        for j in range(NEAR):
            place = jnp.clip(list_ref[i, j] - first, 0, 3 * leaves - 1)
            cols = pl.ds(j * LEAF, LEAF)
            part = dot(near[0, rows, cols], table[place]) + dot(near[1, rows, cols], turned[place])
            total = part if total is None else total + part
        far[rows, :] = total

    def arrivals(s, off_x):
        for off_z in z_offs:
            if off_x == 0 and off_z == 0:
                continue
            from_z = (z + nz - off_z) % nz
            slot = arrived.at[s, pl.ds(pl.multiple_of(from_z * RANK, RANK), RANK)]
            pltpu.make_async_copy(slot, slot, a_recv.at[s, from_z]).wait()
        load_mid[s].wait()
        tz[...] = turn(arrived[s])

    b_copies = []
    tile = nc * RANK
    for s, off_x in enumerate(x_offs):
        arrivals(s, off_x)
        for t, off_y in enumerate(y_offs):
            to_y = (y + off_y) % ny
            rows = pl.ds(pl.multiple_of(to_y * tile, tile), tile)
            part = dot(mid[s, 0, rows, :], arrived[s]) + dot(mid[s, 1, rows, :], tz[...])
            if s > 0:
                part = part + acc[t]
            if s < nx - 1:
                acc[t] = part
                continue
            msend[t] = part.astype(BF16)
            here = pl.ds(pl.multiple_of(core * RANK, RANK), RANK)
            for off_c in c_offs:
                to_c = (core + off_c) % nc
                there = pl.ds(pl.multiple_of(to_c * RANK, RANK), RANK)
                if off_y == 0 and off_c == 0:
                    landed[t, here, :] = msend[t, here, :]
                    continue
                copy = pltpu.make_async_remote_copy(
                    msend.at[t, there],
                    landed.at[t, here],
                    b_send.at[t, to_c],
                    b_recv.at[t, core],
                    device_id=(my_row, to_y * nc + to_c),
                    device_id_type=MESH,
                )
                copy.start()
                b_copies.append(copy)

    order = [ny - 1] + list(range(1, ny - 1)) + [0]
    for place, t in enumerate(order):
        for off_c in c_offs:
            if y_offs[t] == 0 and off_c == 0:
                continue
            from_c = (core + nc - off_c) % nc
            slot = landed.at[t, pl.ds(pl.multiple_of(from_c * RANK, RANK), RANK)]
            pltpu.make_async_copy(slot, slot, b_recv.at[t, from_c]).wait()
        load_row[t].wait()
        data = landed[t]
        part = far[...] + dot(row[t, 0], data) + dot(row[t, 1], turn(data))
        if place < ny - 1:
            far[...] = part
        else:
            out_ref[...] = part.astype(BF16)

    for copy in halo + a_copies + b_copies:
        copy.wait_send()


def on_device(sizes, excitation, near_list, near_blocks, col_factors, coupling, row_factors):
    nx, nz, ny, nc = sizes
    unk, cols = excitation.shape
    dma = pltpu.SemaphoreType.DMA
    hbm = pl.BlockSpec(memory_space=pl.ANY)
    rows_mid = coupling.shape[1]
    moved = sum(a.size * 2 for a in (near_blocks, col_factors, coupling, row_factors))
    return pl.pallas_call(
        functools.partial(kernel, nx, nz, ny, nc),
        out_shape=jax.ShapeDtypeStruct((unk, cols), BF16),
        in_specs=[hbm, pl.BlockSpec(memory_space=pltpu.SMEM), hbm, hbm, hbm, hbm],
        out_specs=pl.BlockSpec(memory_space=pltpu.VMEM),
        scratch_shapes=[
            pltpu.VMEM((3 * unk // LEAF, LEAF, cols), BF16),
            pltpu.VMEM((3 * unk // LEAF, LEAF, cols), BF16),
            pltpu.VMEM(near_blocks.shape, BF16),
            pltpu.VMEM((nx, 2, unk, nz * RANK), BF16),
            pltpu.VMEM((nx, 2, rows_mid, nz * RANK), BF16),
            pltpu.VMEM((ny, 2, unk, nc * RANK), BF16),
            pltpu.VMEM((2, cols, unk), BF16),
            pltpu.VMEM((nx, nz, RANK, cols), BF16),
            pltpu.VMEM((nx, nz * RANK, cols), BF16),
            pltpu.VMEM((nz * RANK, cols), BF16),
            pltpu.VMEM((ny, nc * RANK, cols), F32),
            pltpu.VMEM((ny, nc * RANK, cols), BF16),
            pltpu.VMEM((ny, nc * RANK, cols), BF16),
            pltpu.VMEM((unk, cols), F32),
            dma, dma, dma((nx,)), dma((nx,)), dma((ny,)),
            dma((2,)), dma((2,)), dma((nx, nz)), dma((nx, nz)), dma((ny, nc)), dma((ny, nc)),
        ],
        compiler_params=pltpu.CompilerParams(
            collective_id=0, has_side_effects=True, vmem_limit_bytes=56 * 2**20
        ),
        cost_estimate=pl.CostEstimate(flops=128 * moved, bytes_accessed=moved, transcendentals=0),
    )(excitation.reshape(unk // LEAF, LEAF, cols), near_list, near_blocks, col_factors, coupling, row_factors)


def solution(mesh):
    nx = nz = int(round(mesh.shape["row"] ** 0.5))
    nc = 2
    ny = mesh.shape["col"] // nc
    split = P(("row", "col"), None)
    split3 = P(None, ("row", "col"), None)
    return jax.shard_map(
        functools.partial(on_device, (nx, nz, ny, nc)),
        mesh=mesh,
        in_specs=(split, split, split3, split3, split3, split3),
        out_specs=split,
        check_vma=False,
    )
```

```python
import functools

import jax
import jax.numpy as jnp
from jax import lax
from jax.experimental import pallas as pl
from jax.experimental.pallas import tpu as pltpu
from jax.sharding import PartitionSpec as P

RANK = 128
LEAF = 128
NEAR = 5
MESH = pl.DeviceIdType.MESH
BF16 = jnp.bfloat16
F32 = jnp.float32


def ring_order(count):
    return sorted(range(count), key=lambda k: (-min(k, count - k), k))


def turn(data):
    half = data.shape[1] // 2
    wide = data.astype(F32)
    rolled = pltpu.roll(wide, half, 1)
    lane = lax.broadcasted_iota(jnp.int32, wide.shape, 1)
    return jnp.where(lane < half, -rolled, rolled).astype(BF16)


def dot(a, b):
    return jnp.dot(a, b, preferred_element_type=F32)


def kernel(
    nx, nz, ny, nc,
    x_hbm, list_ref, near_hbm, col_hbm, mid_hbm, row_hbm, out_ref,
    table, turned, near, col, mid, row, xt, csend, arrived, tz, acc, msend, landed, far,
    x_sem, near_sem, col_sem, mid_sem, row_sem,
    halo_send, halo_recv, a_send, a_recv, b_send, b_recv,
):
    leaves = x_hbm.shape[0]
    unk = leaves * LEAF
    my_row, my_col = lax.axis_index("row"), lax.axis_index("col")
    x, z = my_row // nz, my_row % nz
    y, core = my_col // nc, my_col % nc
    n_col, n_all = ny * nc, nx * nz * ny * nc
    x_offs, z_offs, y_offs, c_offs = (ring_order(n) for n in (nx, nz, ny, nc))
    wx, wy = nz * RANK, nc * RANK

    me = my_row * n_col + my_col
    after = (me + 1) % n_all
    before = (me + n_all - 1) % n_all
    after_id = (after // n_col, after % n_col)
    before_id = (before // n_col, before % n_col)

    own = table.at[pl.ds(leaves, leaves)]
    load_x = pltpu.make_async_copy(x_hbm, own, x_sem)
    load_x.start()

    def span(position, width):
        return pl.ds(pl.multiple_of(position * width, width), width)

    load_col = [
        pltpu.make_async_copy(col_hbm.at[:, :, span((x + off) % nx, wx)], col.at[s], col_sem.at[s])
        for s, off in enumerate(x_offs)
    ]
    load_mid = [
        pltpu.make_async_copy(mid_hbm.at[:, :, span((x + nx - off) % nx, wx)], mid.at[s], mid_sem.at[s])
        for s, off in enumerate(x_offs)
    ]
    load_row = [
        pltpu.make_async_copy(row_hbm.at[:, :, span((y + ny - off) % ny, wy)], row.at[t], row_sem.at[t])
        for t, off in enumerate(y_offs)
    ]
    load_near = pltpu.make_async_copy(near_hbm, near, near_sem)
    for copy in load_col:
        copy.start()

    barrier = pltpu.get_barrier_semaphore()
    greeted = 0
    for off_x in range(nx):
        for off_z in range(nz):
            if off_x or off_z:
                peer = ((x + off_x) % nx * nz + (z + off_z) % nz, my_col)
                pl.semaphore_signal(barrier, inc=1, device_id=peer, device_id_type=MESH)
                greeted += 1
    for off in range(1, n_col):
        pl.semaphore_signal(barrier, inc=1, device_id=(my_row, (my_col + off) % n_col), device_id_type=MESH)
        greeted += 1
    for peer in (after_id, before_id):
        pl.semaphore_signal(barrier, inc=1, device_id=peer, device_id_type=MESH)
        greeted += 1

    load_x.wait()
    mine = table[pl.ds(leaves, leaves)].reshape(unk, LEAF)
    flipped = mine.astype(F32).T.astype(BF16)
    half = flipped.shape[0] // 2
    xt[0] = flipped
    xt[1] = jnp.concatenate([-flipped[half:], flipped[:half]], axis=0)
    turned[pl.ds(leaves, leaves)] = turn(mine).reshape(leaves, LEAF, LEAF)

    later = [[load_near], load_mid[:1], load_mid[1:2], load_mid[2:]]
    a_copies = []
    for s, off_x in enumerate(x_offs):
        load_col[s].wait()
        for copy in later[s] if s < len(later) else ():
            copy.start()
        block = dot(xt[0], col[s, 0]) + dot(xt[1], col[s, 1])
        for j in range(nz):
            csend[s, j] = block[:, j * RANK : (j + 1) * RANK].T.astype(BF16)
        if s == 0:
            pl.semaphore_wait(barrier, greeted)
        for off_z in z_offs:
            to_z = (z + off_z) % nz
            if off_x == 0 and off_z == 0:
                arrived[s, pl.ds(pl.multiple_of(z * RANK, RANK), RANK), :] = csend[s, z]
                continue
            copy = pltpu.make_async_remote_copy(
                csend.at[s, to_z],
                arrived.at[s, pl.ds(pl.multiple_of(z * RANK, RANK), RANK)],
                a_send.at[s, to_z],
                a_recv.at[s, z],
                device_id=((x + off_x) % nx * nz + to_z, my_col),
                device_id_type=MESH,
            )
            copy.start()
            a_copies.append(copy)
    for copies in later[len(x_offs) :]:
        for copy in copies:
            copy.start()
    for copy in load_row:
        copy.start()

    halo = [
        pltpu.make_async_remote_copy(
            x_hbm, table.at[pl.ds(0, leaves)], halo_send.at[0], halo_recv.at[0],
            device_id=after_id, device_id_type=MESH,
        ),
        pltpu.make_async_remote_copy(
            x_hbm, table.at[pl.ds(2 * leaves, leaves)], halo_send.at[1], halo_recv.at[1],
            device_id=before_id, device_id_type=MESH,
        ),
    ]
    for copy in halo:
        copy.start()

    def arrivals(s, off_x):
        for off_z in z_offs:
            if off_x == 0 and off_z == 0:
                continue
            from_z = (z + nz - off_z) % nz
            slot = arrived.at[s, pl.ds(pl.multiple_of(from_z * RANK, RANK), RANK)]
            pltpu.make_async_copy(slot, slot, a_recv.at[s, from_z]).wait()
        load_mid[s].wait()
        tz[...] = turn(arrived[s])

    b_copies = []
    tile = nc * RANK
    for s, off_x in enumerate(x_offs):
        arrivals(s, off_x)
        for t, off_y in enumerate(y_offs):
            to_y = (y + off_y) % ny
            rows = pl.ds(pl.multiple_of(to_y * tile, tile), tile)
            part = dot(mid[s, 0, rows, :], arrived[s]) + dot(mid[s, 1, rows, :], tz[...])
            if s > 0:
                part = part + acc[t]
            if s < nx - 1:
                acc[t] = part
                continue
            msend[t] = part.astype(BF16)
            here = pl.ds(pl.multiple_of(core * RANK, RANK), RANK)
            for off_c in c_offs:
                to_c = (core + off_c) % nc
                there = pl.ds(pl.multiple_of(to_c * RANK, RANK), RANK)
                if off_y == 0 and off_c == 0:
                    landed[t, here, :] = msend[t, here, :]
                    continue
                copy = pltpu.make_async_remote_copy(
                    msend.at[t, there],
                    landed.at[t, here],
                    b_send.at[t, to_c],
                    b_recv.at[t, core],
                    device_id=(my_row, to_y * nc + to_c),
                    device_id_type=MESH,
                )
                copy.start()
                b_copies.append(copy)

    for copy in halo:
        copy.wait_recv()
    load_near.wait()
    for start in (0, 2 * leaves):
        side = table[pl.ds(start, leaves)].reshape(unk, LEAF)
        turned[pl.ds(start, leaves)] = turn(side).reshape(leaves, LEAF, LEAF)
    first = me * leaves - leaves
    for i in range(leaves):
        total = None
        rows = pl.ds(i * LEAF, LEAF)
        for j in range(NEAR):
            place = jnp.clip(list_ref[i, j] - first, 0, 3 * leaves - 1)
            cols = pl.ds(j * LEAF, LEAF)
            part = dot(near[0, rows, cols], table[place]) + dot(near[1, rows, cols], turned[place])
            total = part if total is None else total + part
        far[rows, :] = total

    for t in range(ny):
        for off_c in c_offs:
            if y_offs[t] == 0 and off_c == 0:
                continue
            from_c = (core + nc - off_c) % nc
            slot = landed.at[t, pl.ds(pl.multiple_of(from_c * RANK, RANK), RANK)]
            pltpu.make_async_copy(slot, slot, b_recv.at[t, from_c]).wait()
        load_row[t].wait()
    turns = [turn(landed[t]) for t in range(ny)]
    for i in range(unk // 1024):
        rows = pl.ds(i * 1024, 1024)
        part = far[rows, :]
        for t in range(ny):
            part = part + dot(row[t, 0, rows, :], landed[t]) + dot(row[t, 1, rows, :], turns[t])
        out_ref[rows, :] = part.astype(BF16)

    for copy in halo + a_copies + b_copies:
        copy.wait_send()


def put_out(data_ref, out_ref, sem):
    copy = pltpu.make_async_copy(data_ref, out_ref, sem)
    copy.start()
    copy.wait()


def on_device(sizes, excitation, near_list, near_blocks, col_factors, coupling, row_factors):
    nx, nz, ny, nc = sizes
    unk, cols = excitation.shape
    dma = pltpu.SemaphoreType.DMA
    hbm = pl.BlockSpec(memory_space=pl.ANY)
    rows_mid = coupling.shape[1]
    moved = sum(a.size * 2 for a in (near_blocks, col_factors, coupling, row_factors))
    response = pl.pallas_call(
        functools.partial(kernel, nx, nz, ny, nc),
        out_shape=pltpu.VMEM((unk, cols), BF16),
        in_specs=[hbm, pl.BlockSpec(memory_space=pltpu.SMEM), hbm, hbm, hbm, hbm],
        out_specs=pl.BlockSpec(memory_space=pltpu.VMEM),
        scratch_shapes=[
            pltpu.VMEM((3 * unk // LEAF, LEAF, cols), BF16),
            pltpu.VMEM((3 * unk // LEAF, LEAF, cols), BF16),
            pltpu.VMEM(near_blocks.shape, BF16),
            pltpu.VMEM((nx, 2, unk, nz * RANK), BF16),
            pltpu.VMEM((nx, 2, rows_mid, nz * RANK), BF16),
            pltpu.VMEM((ny, 2, unk, nc * RANK), BF16),
            pltpu.VMEM((2, cols, unk), BF16),
            pltpu.VMEM((nx, nz, RANK, cols), BF16),
            pltpu.VMEM((nx, nz * RANK, cols), BF16),
            pltpu.VMEM((nz * RANK, cols), BF16),
            pltpu.VMEM((ny, nc * RANK, cols), F32),
            pltpu.VMEM((ny, nc * RANK, cols), BF16),
            pltpu.VMEM((ny, nc * RANK, cols), BF16),
            pltpu.VMEM((unk, cols), F32),
            dma, dma, dma((nx,)), dma((nx,)), dma((ny,)),
            dma((2,)), dma((2,)), dma((nx, nz)), dma((nx, nz)), dma((ny, nc)), dma((ny, nc)),
        ],
        compiler_params=pltpu.CompilerParams(
            collective_id=0, has_side_effects=True, vmem_limit_bytes=56 * 2**20
        ),
        cost_estimate=pl.CostEstimate(flops=128 * moved, bytes_accessed=moved, transcendentals=0),
    )(excitation.reshape(unk // LEAF, LEAF, cols), near_list, near_blocks, col_factors, coupling, row_factors)
    return response


def solution(mesh):
    nx = nz = int(round(mesh.shape["row"] ** 0.5))
    nc = 2
    ny = mesh.shape["col"] // nc
    split = P(("row", "col"), None)
    split3 = P(None, ("row", "col"), None)
    return jax.shard_map(
        functools.partial(on_device, (nx, nz, ny, nc)),
        mesh=mesh,
        in_specs=(split, split, split3, split3, split3, split3),
        out_specs=split,
        check_vma=False,
    )
```

```python
import functools

import jax
import jax.numpy as jnp
from jax import lax
from jax.experimental import pallas as pl
from jax.experimental.pallas import tpu as pltpu
from jax.sharding import PartitionSpec as P

RANK = 128
LEAF = 128
NEAR = 5
MESH = pl.DeviceIdType.MESH
BF16 = jnp.bfloat16
F32 = jnp.float32


def ring_order(count):
    return sorted(range(count), key=lambda k: (-min(k, count - k), k))


def turn(data):
    half = data.shape[1] // 2
    wide = data.astype(F32)
    rolled = pltpu.roll(wide, half, 1)
    lane = lax.broadcasted_iota(jnp.int32, wide.shape, 1)
    return jnp.where(lane < half, -rolled, rolled).astype(BF16)


def dot(a, b):
    return jnp.dot(a, b, preferred_element_type=F32)


def kernel(
    nx, nz, ny, nc,
    x_hbm, list_hbm, near_hbm, col_hbm, mid_hbm, row_hbm, out_ref,
    list_ref, table, turned, near, col, mid, row, xt, csend, arrived, tz, acc, msend, landed, far,
    list_sem, x_sem, near_sem, col_sem, mid_sem, row_sem,
    halo_send, halo_recv, a_send, a_recv, b_send, b_recv,
):
    leaves = x_hbm.shape[0]
    unk = leaves * LEAF
    my_row, my_col = lax.axis_index("row"), lax.axis_index("col")
    x, z = my_row // nz, my_row % nz
    y, core = my_col // nc, my_col % nc
    n_col, n_all = ny * nc, nx * nz * ny * nc
    x_offs, z_offs, y_offs, c_offs = (ring_order(n) for n in (nx, nz, ny, nc))
    wx, wy = nz * RANK, nc * RANK

    me = my_row * n_col + my_col
    after = (me + 1) % n_all
    before = (me + n_all - 1) % n_all
    after_id = (after // n_col, after % n_col)
    before_id = (before // n_col, before % n_col)

    own = table.at[pl.ds(leaves, leaves)]
    load_x = pltpu.make_async_copy(x_hbm, own, x_sem)
    load_x.start()

    def span(position, width):
        return pl.ds(pl.multiple_of(position * width, width), width)

    load_col = [
        pltpu.make_async_copy(col_hbm.at[:, :, span((x + off) % nx, wx)], col.at[s], col_sem.at[s])
        for s, off in enumerate(x_offs)
    ]
    load_mid = [
        pltpu.make_async_copy(mid_hbm.at[:, :, span((x + nx - off) % nx, wx)], mid.at[s], mid_sem.at[s])
        for s, off in enumerate(x_offs)
    ]
    load_row = [
        pltpu.make_async_copy(row_hbm.at[:, :, span((y + ny - off) % ny, wy)], row.at[t], row_sem.at[t])
        for t, off in enumerate(y_offs)
    ]
    load_near = pltpu.make_async_copy(near_hbm, near, near_sem)
    for copy in load_col:
        copy.start()

    barrier = pltpu.get_barrier_semaphore()
    greeted = 0
    for off_x in range(nx):
        for off_z in range(nz):
            if off_x or off_z:
                peer = ((x + off_x) % nx * nz + (z + off_z) % nz, my_col)
                pl.semaphore_signal(barrier, inc=1, device_id=peer, device_id_type=MESH)
                greeted += 1
    for off in range(1, n_col):
        pl.semaphore_signal(barrier, inc=1, device_id=(my_row, (my_col + off) % n_col), device_id_type=MESH)
        greeted += 1
    for peer in (after_id, before_id):
        pl.semaphore_signal(barrier, inc=1, device_id=peer, device_id_type=MESH)
        greeted += 1

    load_x.wait()
    mine = table[pl.ds(leaves, leaves)].reshape(unk, LEAF)
    flipped = mine.astype(F32).T.astype(BF16)
    half = flipped.shape[0] // 2
    xt[0] = flipped
    xt[1] = jnp.concatenate([-flipped[half:], flipped[:half]], axis=0)

    load_list = pltpu.make_async_copy(list_hbm, list_ref, list_sem)
    later = [[load_list, load_near], load_mid[:1], load_mid[1:2], load_mid[2:]]
    a_copies = []
    for s, off_x in enumerate(x_offs):
        load_col[s].wait()
        for copy in later[s] if s < len(later) else ():
            copy.start()
        block = dot(xt[0], col[s, 0]) + dot(xt[1], col[s, 1])
        for j in range(nz):
            csend[s, j] = block[:, j * RANK : (j + 1) * RANK].T.astype(BF16)
        if s == 0:
            pl.semaphore_wait(barrier, greeted)
        for off_z in z_offs:
            to_z = (z + off_z) % nz
            if off_x == 0 and off_z == 0:
                arrived[s, pl.ds(pl.multiple_of(z * RANK, RANK), RANK), :] = csend[s, z]
                continue
            copy = pltpu.make_async_remote_copy(
                csend.at[s, to_z],
                arrived.at[s, pl.ds(pl.multiple_of(z * RANK, RANK), RANK)],
                a_send.at[s, to_z],
                a_recv.at[s, z],
                device_id=((x + off_x) % nx * nz + to_z, my_col),
                device_id_type=MESH,
            )
            copy.start()
            a_copies.append(copy)
    for copies in later[len(x_offs) :]:
        for copy in copies:
            copy.start()
    for copy in load_row:
        copy.start()

    halo = [
        pltpu.make_async_remote_copy(
            x_hbm, table.at[pl.ds(0, leaves)], halo_send.at[0], halo_recv.at[0],
            device_id=after_id, device_id_type=MESH,
        ),
        pltpu.make_async_remote_copy(
            x_hbm, table.at[pl.ds(2 * leaves, leaves)], halo_send.at[1], halo_recv.at[1],
            device_id=before_id, device_id_type=MESH,
        ),
    ]
    for copy in halo:
        copy.start()

    def arrivals(s, off_x):
        for off_z in z_offs:
            if off_x == 0 and off_z == 0:
                continue
            from_z = (z + nz - off_z) % nz
            slot = arrived.at[s, pl.ds(pl.multiple_of(from_z * RANK, RANK), RANK)]
            pltpu.make_async_copy(slot, slot, a_recv.at[s, from_z]).wait()
        load_mid[s].wait()
        tz[...] = turn(arrived[s])

    b_copies = []
    tile = nc * RANK
    for s, off_x in enumerate(x_offs):
        arrivals(s, off_x)
        for t, off_y in enumerate(y_offs):
            to_y = (y + off_y) % ny
            rows = pl.ds(pl.multiple_of(to_y * tile, tile), tile)
            part = dot(mid[s, 0, rows, :], arrived[s]) + dot(mid[s, 1, rows, :], tz[...])
            if s > 0:
                part = part + acc[t]
            if s < nx - 1:
                acc[t] = part
                continue
            msend[t] = part.astype(BF16)
            here = pl.ds(pl.multiple_of(core * RANK, RANK), RANK)
            for off_c in c_offs:
                to_c = (core + off_c) % nc
                there = pl.ds(pl.multiple_of(to_c * RANK, RANK), RANK)
                if off_y == 0 and off_c == 0:
                    landed[t, here, :] = msend[t, here, :]
                    continue
                copy = pltpu.make_async_remote_copy(
                    msend.at[t, there],
                    landed.at[t, here],
                    b_send.at[t, to_c],
                    b_recv.at[t, core],
                    device_id=(my_row, to_y * nc + to_c),
                    device_id_type=MESH,
                )
                copy.start()
                b_copies.append(copy)

    for copy in halo:
        copy.wait_recv()
    load_near.wait()
    load_list.wait()
    for start in (0, leaves, 2 * leaves):
        side = table[pl.ds(start, leaves)].reshape(unk, LEAF)
        turned[pl.ds(start, leaves)] = turn(side).reshape(leaves, LEAF, LEAF)
    first = me * leaves - leaves
    for i in range(leaves):
        total = None
        rows = pl.ds(i * LEAF, LEAF)
        for j in range(NEAR):
            place = jnp.clip(list_ref[i, j] - first, 0, 3 * leaves - 1)
            cols = pl.ds(j * LEAF, LEAF)
            part = dot(near[0, rows, cols], table[place]) + dot(near[1, rows, cols], turned[place])
            total = part if total is None else total + part
        far[rows, :] = total

    def landing(t):
        for off_c in c_offs:
            if y_offs[t] == 0 and off_c == 0:
                continue
            from_c = (core + nc - off_c) % nc
            slot = landed.at[t, pl.ds(pl.multiple_of(from_c * RANK, RANK), RANK)]
            pltpu.make_async_copy(slot, slot, b_recv.at[t, from_c]).wait()
        load_row[t].wait()

    landing(ny - 1)
    far[...] += dot(row[ny - 1, 0], landed[ny - 1]) + dot(row[ny - 1, 1], turn(landed[ny - 1]))
    for t in range(ny - 1):
        landing(t)
    part = far[...]
    for t in range(ny - 1):
        part = part + dot(row[t, 0], landed[t]) + dot(row[t, 1], turn(landed[t]))
    out_ref[...] = part.astype(BF16)

    for copy in halo + a_copies + b_copies:
        copy.wait_send()


def put_out(data_ref, out_ref, sem):
    copy = pltpu.make_async_copy(data_ref, out_ref, sem)
    copy.start()
    copy.wait()


def on_device(sizes, excitation, near_list, near_blocks, col_factors, coupling, row_factors):
    nx, nz, ny, nc = sizes
    unk, cols = excitation.shape
    dma = pltpu.SemaphoreType.DMA
    hbm = pl.BlockSpec(memory_space=pl.ANY)
    rows_mid = coupling.shape[1]
    moved = sum(a.size * 2 for a in (near_blocks, col_factors, coupling, row_factors))
    response = pl.pallas_call(
        functools.partial(kernel, nx, nz, ny, nc),
        out_shape=pltpu.VMEM((unk, cols), BF16),
        in_specs=[hbm, hbm, hbm, hbm, hbm, hbm],
        out_specs=pl.BlockSpec(memory_space=pltpu.VMEM),
        scratch_shapes=[
            pltpu.SMEM(near_list.shape, jnp.int32),
            pltpu.VMEM((3 * unk // LEAF, LEAF, cols), BF16),
            pltpu.VMEM((3 * unk // LEAF, LEAF, cols), BF16),
            pltpu.VMEM(near_blocks.shape, BF16),
            pltpu.VMEM((nx, 2, unk, nz * RANK), BF16),
            pltpu.VMEM((nx, 2, rows_mid, nz * RANK), BF16),
            pltpu.VMEM((ny, 2, unk, nc * RANK), BF16),
            pltpu.VMEM((2, cols, unk), BF16),
            pltpu.VMEM((nx, nz, RANK, cols), BF16),
            pltpu.VMEM((nx, nz * RANK, cols), BF16),
            pltpu.VMEM((nz * RANK, cols), BF16),
            pltpu.VMEM((ny, nc * RANK, cols), F32),
            pltpu.VMEM((ny, nc * RANK, cols), BF16),
            pltpu.VMEM((ny, nc * RANK, cols), BF16),
            pltpu.VMEM((unk, cols), F32),
            dma, dma, dma, dma((nx,)), dma((nx,)), dma((ny,)),
            dma((2,)), dma((2,)), dma((nx, nz)), dma((nx, nz)), dma((ny, nc)), dma((ny, nc)),
        ],
        compiler_params=pltpu.CompilerParams(
            collective_id=0, has_side_effects=True, vmem_limit_bytes=56 * 2**20
        ),
        cost_estimate=pl.CostEstimate(flops=128 * moved, bytes_accessed=moved, transcendentals=0),
    )(excitation.reshape(unk // LEAF, LEAF, cols), near_list, near_blocks, col_factors, coupling, row_factors)
    return response


def solution(mesh):
    nx = nz = int(round(mesh.shape["row"] ** 0.5))
    nc = 2
    ny = mesh.shape["col"] // nc
    split = P(("row", "col"), None)
    split3 = P(None, ("row", "col"), None)
    return jax.shard_map(
        functools.partial(on_device, (nx, nz, ny, nc)),
        mesh=mesh,
        in_specs=(split, split, split3, split3, split3, split3),
        out_specs=split,
        check_vma=False,
    )
```

```python
import functools

import jax
import jax.numpy as jnp
from jax import lax
from jax.experimental import pallas as pl
from jax.experimental.pallas import tpu as pltpu
from jax.sharding import PartitionSpec as P

RANK = 128
LEAF = 128
NEAR = 5
MESH = pl.DeviceIdType.MESH
BF16 = jnp.bfloat16
F32 = jnp.float32


def ring_order(count):
    return sorted(range(count), key=lambda k: (-min(k, count - k), k))


def turn(data):
    half = data.shape[1] // 2
    wide = data.astype(F32)
    rolled = pltpu.roll(wide, half, 1)
    lane = lax.broadcasted_iota(jnp.int32, wide.shape, 1)
    return jnp.where(lane < half, -rolled, rolled).astype(BF16)


def swap(data):
    half = data.shape[0] // 2
    return jnp.concatenate([-data[half:], data[:half]], axis=0)


def dot_t(a, b):
    return lax.dot_general(a, b, (((1,), (1,)), ((), ())), preferred_element_type=F32)


def dot(a, b):
    return jnp.dot(a, b, preferred_element_type=F32)


def kernel(
    nx, nz, ny, nc,
    x_hbm, list_hbm, near_hbm, col_hbm, mid_hbm, row_hbm, out_ref,
    list_ref, table, turned, near, col, mid, row, xt, csend, arrived, mid_t, row_t, acc, msend, landed, far,
    list_sem, x_sem, near_sem, col_sem, mid_sem, row_sem,
    halo_send, halo_recv, a_send, a_recv, b_send, b_recv,
):
    leaves = x_hbm.shape[0]
    unk = leaves * LEAF
    my_row, my_col = lax.axis_index("row"), lax.axis_index("col")
    x, z = my_row // nz, my_row % nz
    y, core = my_col // nc, my_col % nc
    n_col, n_all = ny * nc, nx * nz * ny * nc
    x_offs, z_offs, y_offs, c_offs = (ring_order(n) for n in (nx, nz, ny, nc))
    wx, wy = nz * RANK, nc * RANK

    me = my_row * n_col + my_col
    after = (me + 1) % n_all
    before = (me + n_all - 1) % n_all
    after_id = (after // n_col, after % n_col)
    before_id = (before // n_col, before % n_col)

    own = table.at[pl.ds(leaves, leaves)]
    load_x = pltpu.make_async_copy(x_hbm, own, x_sem)
    load_x.start()

    def span(position, width):
        return pl.ds(pl.multiple_of(position * width, width), width)

    load_col = [
        pltpu.make_async_copy(col_hbm.at[:, :, span((x + off) % nx, wx)], col.at[s], col_sem.at[s])
        for s, off in enumerate(x_offs)
    ]
    load_mid = [
        [
            pltpu.make_async_copy(
                mid_hbm.at[:, span((y + off_y) % ny, wy), span((x + nx - off) % nx, wx)],
                mid.at[s, :, pl.ds(t * wy, wy)],
                mid_sem.at[s, t],
            )
            for t, off_y in enumerate(y_offs)
        ]
        for s, off in enumerate(x_offs)
    ]
    load_row = [
        pltpu.make_async_copy(row_hbm.at[:, :, span((y + ny - off) % ny, wy)], row.at[t], row_sem.at[t])
        for t, off in enumerate(y_offs)
    ]
    load_near = pltpu.make_async_copy(near_hbm, near, near_sem)
    for copy in load_col:
        copy.start()

    barrier = pltpu.get_barrier_semaphore()
    greeted = 0
    for off_x in range(nx):
        for off_z in range(nz):
            if off_x or off_z:
                peer = ((x + off_x) % nx * nz + (z + off_z) % nz, my_col)
                pl.semaphore_signal(barrier, inc=1, device_id=peer, device_id_type=MESH)
                greeted += 1
    for off in range(1, n_col):
        pl.semaphore_signal(barrier, inc=1, device_id=(my_row, (my_col + off) % n_col), device_id_type=MESH)
        greeted += 1
    for peer in (after_id, before_id):
        pl.semaphore_signal(barrier, inc=1, device_id=peer, device_id_type=MESH)
        greeted += 1

    load_x.wait()
    mine = table[pl.ds(leaves, leaves)].reshape(unk, LEAF)
    flipped = mine.astype(F32).T.astype(BF16)
    half = flipped.shape[0] // 2
    xt[0] = flipped
    xt[1] = jnp.concatenate([-flipped[half:], flipped[:half]], axis=0)

    load_list = pltpu.make_async_copy(list_hbm, list_ref, list_sem)
    later = [load_mid[-1], load_row, [load_list, load_near] + load_mid[0], sum(load_mid[1:-1], [])]
    a_copies = []
    for s, off_x in enumerate(x_offs):
        load_col[s].wait()
        for copy in later[s] if s < len(later) else ():
            copy.start()
        block = dot(xt[0], col[s, 0]) + dot(xt[1], col[s, 1])
        for j in range(nz):
            csend[s, j] = block[:, j * RANK : (j + 1) * RANK].astype(BF16)
        if s == 0:
            pl.semaphore_wait(barrier, greeted)
        for off_z in z_offs:
            to_z = (z + off_z) % nz
            if off_x == 0 and off_z == 0:
                arrived[s, z] = csend[s, z]
                continue
            copy = pltpu.make_async_remote_copy(
                csend.at[s, to_z],
                arrived.at[s, z],
                a_send.at[s, to_z],
                a_recv.at[s, z],
                device_id=((x + off_x) % nx * nz + to_z, my_col),
                device_id_type=MESH,
            )
            copy.start()
            a_copies.append(copy)
    for copies in later[len(x_offs) :]:
        for copy in copies:
            copy.start()

    halo = [
        pltpu.make_async_remote_copy(
            x_hbm, table.at[pl.ds(0, leaves)], halo_send.at[0], halo_recv.at[0],
            device_id=after_id, device_id_type=MESH,
        ),
        pltpu.make_async_remote_copy(
            x_hbm, table.at[pl.ds(2 * leaves, leaves)], halo_send.at[1], halo_recv.at[1],
            device_id=before_id, device_id_type=MESH,
        ),
    ]
    for copy in halo:
        copy.start()

    for copy in load_mid[-1]:
        copy.wait()
    for p in range(2):
        mid_t[p] = mid[nx - 1, p].T
    for t in range(ny):
        load_row[t].wait()
        for p in range(2):
            row_t[t, p] = row[t, p].T

    tile = wy
    b_copies = []
    for s, off_x in enumerate(x_offs):
        for off_z in z_offs:
            if off_x == 0 and off_z == 0:
                continue
            from_z = (z + nz - off_z) % nz
            slot = arrived.at[s, from_z]
            pltpu.make_async_copy(slot, slot, a_recv.at[s, from_z]).wait()
        data = jnp.concatenate([arrived[s, j] for j in range(nz)], axis=1)
        flip = swap(data)
        if s < nx - 1:
            for copy in load_mid[s]:
                copy.wait()
            part = dot_t(data, mid[s, 0]) + dot_t(flip, mid[s, 1])
            acc[...] = part if s == 0 else acc[...] + part
            continue
        for t, off_y in enumerate(y_offs):
            to_y = (y + off_y) % ny
            rows = pl.ds(t * tile, tile)
            part = acc[:, rows] + dot(data, mid_t[0, :, rows]) + dot(flip, mid_t[1, :, rows])
            for q in range(nc):
                msend[t, q] = part[:, q * RANK : (q + 1) * RANK].astype(BF16)
            for off_c in c_offs:
                to_c = (core + off_c) % nc
                if off_y == 0 and off_c == 0:
                    landed[t, core] = msend[t, core]
                    continue
                copy = pltpu.make_async_remote_copy(
                    msend.at[t, to_c],
                    landed.at[t, core],
                    b_send.at[t, to_c],
                    b_recv.at[t, core],
                    device_id=(my_row, to_y * nc + to_c),
                    device_id_type=MESH,
                )
                copy.start()
                b_copies.append(copy)

    for copy in halo:
        copy.wait_recv()
    load_near.wait()
    load_list.wait()
    for start in (0, leaves, 2 * leaves):
        side = table[pl.ds(start, leaves)].reshape(unk, LEAF)
        turned[pl.ds(start, leaves)] = turn(side).reshape(leaves, LEAF, LEAF)
    first = me * leaves - leaves
    for i in range(leaves):
        total = None
        rows = pl.ds(i * LEAF, LEAF)
        for j in range(NEAR):
            place = jnp.clip(list_ref[i, j] - first, 0, 3 * leaves - 1)
            cols = pl.ds(j * LEAF, LEAF)
            part = dot(near[0, rows, cols], table[place]) + dot(near[1, rows, cols], turned[place])
            total = part if total is None else total + part
        far[rows, :] = total

    def landing(t):
        for off_c in c_offs:
            if y_offs[t] == 0 and off_c == 0:
                continue
            from_c = (core + nc - off_c) % nc
            slot = landed.at[t, from_c]
            pltpu.make_async_copy(slot, slot, b_recv.at[t, from_c]).wait()

    def expand(t):
        data = jnp.concatenate([landed[t, q] for q in range(nc)], axis=1)
        return dot(data, row_t[t, 0]) + dot(swap(data), row_t[t, 1])

    landing(ny - 1)
    part = expand(ny - 1)
    for i in range(leaves):
        far[pl.ds(i * LEAF, LEAF), :] += part[:, i * LEAF : (i + 1) * LEAF].T
    for t in range(ny - 1):
        landing(t)
    part = sum(expand(t) for t in range(ny - 1))
    for i in range(leaves):
        rows = pl.ds(i * LEAF, LEAF)
        out_ref[rows, :] = (far[rows, :] + part[:, i * LEAF : (i + 1) * LEAF].T).astype(BF16)

    for copy in halo + a_copies + b_copies:
        copy.wait_send()


def put_out(data_ref, out_ref, sem):
    copy = pltpu.make_async_copy(data_ref, out_ref, sem)
    copy.start()
    copy.wait()


def on_device(sizes, excitation, near_list, near_blocks, col_factors, coupling, row_factors):
    nx, nz, ny, nc = sizes
    unk, cols = excitation.shape
    dma = pltpu.SemaphoreType.DMA
    hbm = pl.BlockSpec(memory_space=pl.ANY)
    rows_mid = coupling.shape[1]
    moved = sum(a.size * 2 for a in (near_blocks, col_factors, coupling, row_factors))
    response = pl.pallas_call(
        functools.partial(kernel, nx, nz, ny, nc),
        out_shape=pltpu.VMEM((unk, cols), BF16),
        in_specs=[hbm, hbm, hbm, hbm, hbm, hbm],
        out_specs=pl.BlockSpec(memory_space=pltpu.VMEM),
        scratch_shapes=[
            pltpu.SMEM(near_list.shape, jnp.int32),
            pltpu.VMEM((3 * unk // LEAF, LEAF, cols), BF16),
            pltpu.VMEM((3 * unk // LEAF, LEAF, cols), BF16),
            pltpu.VMEM(near_blocks.shape, BF16),
            pltpu.VMEM((nx, 2, unk, nz * RANK), BF16),
            pltpu.VMEM((nx, 2, rows_mid, nz * RANK), BF16),
            pltpu.VMEM((ny, 2, unk, nc * RANK), BF16),
            pltpu.VMEM((2, cols, unk), BF16),
            pltpu.VMEM((nx, nz, cols, RANK), BF16),
            pltpu.VMEM((nx, nz, cols, RANK), BF16),
            pltpu.VMEM((2, nz * RANK, rows_mid), BF16),
            pltpu.VMEM((ny, 2, nc * RANK, unk), BF16),
            pltpu.VMEM((cols, rows_mid), F32),
            pltpu.VMEM((ny, nc, cols, RANK), BF16),
            pltpu.VMEM((ny, nc, cols, RANK), BF16),
            pltpu.VMEM((unk, cols), F32),
            dma, dma, dma, dma((nx,)), dma((nx, ny)), dma((ny,)),
            dma((2,)), dma((2,)), dma((nx, nz)), dma((nx, nz)), dma((ny, nc)), dma((ny, nc)),
        ],
        compiler_params=pltpu.CompilerParams(
            collective_id=0, has_side_effects=True, vmem_limit_bytes=56 * 2**20
        ),
        cost_estimate=pl.CostEstimate(flops=128 * moved, bytes_accessed=moved, transcendentals=0),
    )(excitation.reshape(unk // LEAF, LEAF, cols), near_list, near_blocks, col_factors, coupling, row_factors)
    return response


def solution(mesh):
    nx = nz = int(round(mesh.shape["row"] ** 0.5))
    nc = 2
    ny = mesh.shape["col"] // nc
    split = P(("row", "col"), None)
    split3 = P(None, ("row", "col"), None)
    return jax.shard_map(
        functools.partial(on_device, (nx, nz, ny, nc)),
        mesh=mesh,
        in_specs=(split, split, split3, split3, split3, split3),
        out_specs=split,
        check_vma=False,
    )
```

```python
import functools

import jax
import jax.numpy as jnp
from jax import lax
from jax.experimental import pallas as pl
from jax.experimental.pallas import tpu as pltpu
from jax.sharding import PartitionSpec as P

RANK = 128
LEAF = 128
NEAR = 5
MESH = pl.DeviceIdType.MESH
BF16 = jnp.bfloat16
F32 = jnp.float32


def ring_order(count):
    return sorted(range(count), key=lambda k: (-min(k, count - k), k))


def turn(data):
    half = data.shape[1] // 2
    wide = data.astype(F32)
    rolled = pltpu.roll(wide, half, 1)
    lane = lax.broadcasted_iota(jnp.int32, wide.shape, 1)
    return jnp.where(lane < half, -rolled, rolled).astype(BF16)


def swap(data):
    half = data.shape[0] // 2
    return jnp.concatenate([-data[half:], data[:half]], axis=0)


def dot_t(a, b):
    return lax.dot_general(a, b, (((1,), (1,)), ((), ())), preferred_element_type=F32)


def dot(a, b):
    return jnp.dot(a, b, preferred_element_type=F32)


def kernel(
    nx, nz, ny, nc,
    x_hbm, list_hbm, near_hbm, col_hbm, mid_hbm, row_hbm, out_ref,
    list_ref, table, turned, near, col, mid, row, xt, csend, arrived, mid_t, row_t, acc, msend, landed, far,
    list_sem, x_sem, near_sem, col_sem, mid_sem, row_sem,
    halo_send, halo_recv, a_send, a_recv, b_send, b_recv,
):
    leaves = x_hbm.shape[0]
    unk = leaves * LEAF
    my_row, my_col = lax.axis_index("row"), lax.axis_index("col")
    x, z = my_row // nz, my_row % nz
    y, core = my_col // nc, my_col % nc
    n_col, n_all = ny * nc, nx * nz * ny * nc
    x_offs, z_offs, y_offs, c_offs = (ring_order(n) for n in (nx, nz, ny, nc))
    wx, wy = nz * RANK, nc * RANK

    me = my_row * n_col + my_col
    after = (me + 1) % n_all
    before = (me + n_all - 1) % n_all
    after_id = (after // n_col, after % n_col)
    before_id = (before // n_col, before % n_col)

    own = table.at[pl.ds(leaves, leaves)]
    load_x = pltpu.make_async_copy(x_hbm, own, x_sem)
    load_x.start()

    def span(position, width):
        return pl.ds(pl.multiple_of(position * width, width), width)

    load_col = [
        pltpu.make_async_copy(col_hbm.at[:, :, span((x + off) % nx, wx)], col.at[s], col_sem.at[s])
        for s, off in enumerate(x_offs)
    ]
    load_mid = [
        [
            pltpu.make_async_copy(
                mid_hbm.at[:, span((y + off_y) % ny, wy), span((x + nx - off) % nx, wx)],
                mid.at[s, :, pl.ds(t * wy, wy)],
                mid_sem.at[s, t],
            )
            for t, off_y in enumerate(y_offs)
        ]
        for s, off in enumerate(x_offs)
    ]
    load_row = [
        pltpu.make_async_copy(row_hbm.at[:, :, span((y + ny - off) % ny, wy)], row.at[t], row_sem.at[t])
        for t, off in enumerate(y_offs)
    ]
    load_near = pltpu.make_async_copy(near_hbm, near, near_sem)
    for copy in load_col:
        copy.start()

    barrier = pltpu.get_barrier_semaphore()
    greeted = 0
    for off_x in range(nx):
        for off_z in range(nz):
            if off_x or off_z:
                peer = ((x + off_x) % nx * nz + (z + off_z) % nz, my_col)
                pl.semaphore_signal(barrier, inc=1, device_id=peer, device_id_type=MESH)
                greeted += 1
    for off in range(1, n_col):
        pl.semaphore_signal(barrier, inc=1, device_id=(my_row, (my_col + off) % n_col), device_id_type=MESH)
        greeted += 1
    for peer in (after_id, before_id):
        pl.semaphore_signal(barrier, inc=1, device_id=peer, device_id_type=MESH)
        greeted += 1

    load_x.wait()
    mine = table[pl.ds(leaves, leaves)].reshape(unk, LEAF)
    flipped = mine.astype(F32).T.astype(BF16)
    half = flipped.shape[0] // 2
    xt[0] = flipped
    xt[1] = jnp.concatenate([-flipped[half:], flipped[:half]], axis=0)

    load_list = pltpu.make_async_copy(list_hbm, list_ref, list_sem)
    later = [load_mid[-1], load_row, [load_list, load_near] + load_mid[0], sum(load_mid[1:-1], [])]
    a_copies = []
    for s, off_x in enumerate(x_offs):
        load_col[s].wait()
        for copy in later[s] if s < len(later) else ():
            copy.start()
        block = dot(xt[0], col[s, 0]) + dot(xt[1], col[s, 1])
        for j in range(nz):
            csend[s, j] = block[:, j * RANK : (j + 1) * RANK].astype(BF16)
        if s == 0:
            pl.semaphore_wait(barrier, greeted)
        for off_z in z_offs:
            to_z = (z + off_z) % nz
            if off_x == 0 and off_z == 0:
                arrived[s, z] = csend[s, z]
                continue
            copy = pltpu.make_async_remote_copy(
                csend.at[s, to_z],
                arrived.at[s, z],
                a_send.at[s, to_z],
                a_recv.at[s, z],
                device_id=((x + off_x) % nx * nz + to_z, my_col),
                device_id_type=MESH,
            )
            copy.start()
            a_copies.append(copy)
    for copies in later[len(x_offs) :]:
        for copy in copies:
            copy.start()

    for copy in load_mid[-1]:
        copy.wait()
    for p in range(2):
        mid_t[p] = mid[nx - 1, p].T
    for t in range(ny):
        load_row[t].wait()
        for p in range(2):
            row_t[t, p] = row[t, p].T

    tile = wy
    b_copies = []
    for s, off_x in enumerate(x_offs):
        if s == 1:
            halo = [
                pltpu.make_async_remote_copy(
                    x_hbm, table.at[pl.ds(0, leaves)], halo_send.at[0], halo_recv.at[0],
                    device_id=after_id, device_id_type=MESH,
                ),
                pltpu.make_async_remote_copy(
                    x_hbm, table.at[pl.ds(2 * leaves, leaves)], halo_send.at[1], halo_recv.at[1],
                    device_id=before_id, device_id_type=MESH,
                ),
            ]
            for copy in halo:
                copy.start()
        for off_z in z_offs:
            if off_x == 0 and off_z == 0:
                continue
            from_z = (z + nz - off_z) % nz
            slot = arrived.at[s, from_z]
            pltpu.make_async_copy(slot, slot, a_recv.at[s, from_z]).wait()
        data = jnp.concatenate([arrived[s, j] for j in range(nz)], axis=1)
        flip = swap(data)
        if s < nx - 1:
            for copy in load_mid[s]:
                copy.wait()
            part = dot_t(data, mid[s, 0]) + dot_t(flip, mid[s, 1])
            acc[...] = part if s == 0 else acc[...] + part
            continue
        for t, off_y in enumerate(y_offs):
            to_y = (y + off_y) % ny
            rows = pl.ds(t * tile, tile)
            part = acc[:, rows] + dot(data, mid_t[0, :, rows]) + dot(flip, mid_t[1, :, rows])
            for q in range(nc):
                msend[t, q] = part[:, q * RANK : (q + 1) * RANK].astype(BF16)
            for off_c in c_offs:
                to_c = (core + off_c) % nc
                if off_y == 0 and off_c == 0:
                    landed[t, core] = msend[t, core]
                    continue
                copy = pltpu.make_async_remote_copy(
                    msend.at[t, to_c],
                    landed.at[t, core],
                    b_send.at[t, to_c],
                    b_recv.at[t, core],
                    device_id=(my_row, to_y * nc + to_c),
                    device_id_type=MESH,
                )
                copy.start()
                b_copies.append(copy)

    for copy in halo:
        copy.wait_recv()
    load_near.wait()
    load_list.wait()
    for start in (0, leaves, 2 * leaves):
        side = table[pl.ds(start, leaves)].reshape(unk, LEAF)
        turned[pl.ds(start, leaves)] = turn(side).reshape(leaves, LEAF, LEAF)
    first = me * leaves - leaves
    for i in range(leaves):
        total = None
        rows = pl.ds(i * LEAF, LEAF)
        for j in range(NEAR):
            place = jnp.clip(list_ref[i, j] - first, 0, 3 * leaves - 1)
            cols = pl.ds(j * LEAF, LEAF)
            part = dot(near[0, rows, cols], table[place]) + dot(near[1, rows, cols], turned[place])
            total = part if total is None else total + part
        far[rows, :] = total

    def landing(t):
        for off_c in c_offs:
            if y_offs[t] == 0 and off_c == 0:
                continue
            from_c = (core + nc - off_c) % nc
            slot = landed.at[t, from_c]
            pltpu.make_async_copy(slot, slot, b_recv.at[t, from_c]).wait()

    def expand(t):
        data = jnp.concatenate([landed[t, q] for q in range(nc)], axis=1)
        return dot(data, row_t[t, 0]) + dot(swap(data), row_t[t, 1])

    landing(ny - 1)
    part = expand(ny - 1)
    for i in range(leaves):
        far[pl.ds(i * LEAF, LEAF), :] += part[:, i * LEAF : (i + 1) * LEAF].T
    for t in range(ny - 1):
        landing(t)
    part = sum(expand(t) for t in range(ny - 1))
    for i in range(leaves):
        rows = pl.ds(i * LEAF, LEAF)
        out_ref[rows, :] = (far[rows, :] + part[:, i * LEAF : (i + 1) * LEAF].T).astype(BF16)

    for copy in halo + a_copies + b_copies:
        copy.wait_send()


def put_out(data_ref, out_ref, sem):
    copy = pltpu.make_async_copy(data_ref, out_ref, sem)
    copy.start()
    copy.wait()


def on_device(sizes, excitation, near_list, near_blocks, col_factors, coupling, row_factors):
    nx, nz, ny, nc = sizes
    unk, cols = excitation.shape
    dma = pltpu.SemaphoreType.DMA
    hbm = pl.BlockSpec(memory_space=pl.ANY)
    rows_mid = coupling.shape[1]
    moved = sum(a.size * 2 for a in (near_blocks, col_factors, coupling, row_factors))
    response = pl.pallas_call(
        functools.partial(kernel, nx, nz, ny, nc),
        out_shape=pltpu.VMEM((unk, cols), BF16),
        in_specs=[hbm, hbm, hbm, hbm, hbm, hbm],
        out_specs=pl.BlockSpec(memory_space=pltpu.VMEM),
        scratch_shapes=[
            pltpu.SMEM(near_list.shape, jnp.int32),
            pltpu.VMEM((3 * unk // LEAF, LEAF, cols), BF16),
            pltpu.VMEM((3 * unk // LEAF, LEAF, cols), BF16),
            pltpu.VMEM(near_blocks.shape, BF16),
            pltpu.VMEM((nx, 2, unk, nz * RANK), BF16),
            pltpu.VMEM((nx, 2, rows_mid, nz * RANK), BF16),
            pltpu.VMEM((ny, 2, unk, nc * RANK), BF16),
            pltpu.VMEM((2, cols, unk), BF16),
            pltpu.VMEM((nx, nz, cols, RANK), BF16),
            pltpu.VMEM((nx, nz, cols, RANK), BF16),
            pltpu.VMEM((2, nz * RANK, rows_mid), BF16),
            pltpu.VMEM((ny, 2, nc * RANK, unk), BF16),
            pltpu.VMEM((cols, rows_mid), F32),
            pltpu.VMEM((ny, nc, cols, RANK), BF16),
            pltpu.VMEM((ny, nc, cols, RANK), BF16),
            pltpu.VMEM((unk, cols), F32),
            dma, dma, dma, dma((nx,)), dma((nx, ny)), dma((ny,)),
            dma((2,)), dma((2,)), dma((nx, nz)), dma((nx, nz)), dma((ny, nc)), dma((ny, nc)),
        ],
        compiler_params=pltpu.CompilerParams(
            collective_id=0, has_side_effects=True, vmem_limit_bytes=56 * 2**20
        ),
        cost_estimate=pl.CostEstimate(flops=128 * moved, bytes_accessed=moved, transcendentals=0),
    )(excitation.reshape(unk // LEAF, LEAF, cols), near_list, near_blocks, col_factors, coupling, row_factors)
    return response


def solution(mesh):
    nx = nz = int(round(mesh.shape["row"] ** 0.5))
    nc = 2
    ny = mesh.shape["col"] // nc
    split = P(("row", "col"), None)
    split3 = P(None, ("row", "col"), None)
    return jax.shard_map(
        functools.partial(on_device, (nx, nz, ny, nc)),
        mesh=mesh,
        in_specs=(split, split, split3, split3, split3, split3),
        out_specs=split,
        check_vma=False,
    )
```

```python
import functools

import jax
import jax.numpy as jnp
from jax import lax
from jax.experimental import pallas as pl
from jax.experimental.pallas import tpu as pltpu
from jax.sharding import PartitionSpec as P

RANK = 128
LEAF = 128
NEAR = 5
MESH = pl.DeviceIdType.MESH
BF16 = jnp.bfloat16
F32 = jnp.float32


def ring_order(count):
    return sorted(range(count), key=lambda k: (-min(k, count - k), k))


def turn(data):
    half = data.shape[1] // 2
    wide = data.astype(F32)
    rolled = pltpu.roll(wide, half, 1)
    lane = lax.broadcasted_iota(jnp.int32, wide.shape, 1)
    return jnp.where(lane < half, -rolled, rolled).astype(BF16)


def swap(data):
    half = data.shape[0] // 2
    return jnp.concatenate([-data[half:], data[:half]], axis=0)


def dot_t(a, b):
    return lax.dot_general(a, b, (((1,), (1,)), ((), ())), preferred_element_type=F32)


def dot(a, b):
    return jnp.dot(a, b, preferred_element_type=F32)


def kernel(
    nx, nz, ny, nc,
    x_hbm, list_hbm, near_hbm, col_hbm, mid_hbm, row_hbm, out_ref,
    list_ref, table, turned, near, col, mid, row, xt, csend, arrived, mid_t, row_t, acc, msend, landed, far,
    list_sem, x_sem, near_sem, col_sem, mid_sem, row_sem,
    halo_send, halo_recv, a_send, a_recv, b_send, b_recv,
):
    leaves = x_hbm.shape[0]
    unk = leaves * LEAF
    my_row, my_col = lax.axis_index("row"), lax.axis_index("col")
    x, z = my_row // nz, my_row % nz
    y, core = my_col // nc, my_col % nc
    n_col, n_all = ny * nc, nx * nz * ny * nc
    x_offs, z_offs, y_offs, c_offs = (ring_order(n) for n in (nx, nz, ny, nc))
    wx, wy = nz * RANK, nc * RANK

    me = my_row * n_col + my_col
    after = (me + 1) % n_all
    before = (me + n_all - 1) % n_all
    after_id = (after // n_col, after % n_col)
    before_id = (before // n_col, before % n_col)

    own = table.at[pl.ds(leaves, leaves)]
    load_x = pltpu.make_async_copy(x_hbm, own, x_sem)
    load_x.start()

    def span(position, width):
        return pl.ds(pl.multiple_of(position * width, width), width)

    load_col = [
        pltpu.make_async_copy(col_hbm.at[:, :, span((x + off) % nx, wx)], col.at[s], col_sem.at[s])
        for s, off in enumerate(x_offs)
    ]
    load_mid = [
        [
            pltpu.make_async_copy(
                mid_hbm.at[:, span((y + off_y) % ny, wy), span((x + nx - off) % nx, wx)],
                mid.at[s, :, pl.ds(t * wy, wy)],
                mid_sem.at[s, t],
            )
            for t, off_y in enumerate(y_offs)
        ]
        for s, off in enumerate(x_offs)
    ]
    load_row = [
        pltpu.make_async_copy(row_hbm.at[:, :, span((y + ny - off) % ny, wy)], row.at[t], row_sem.at[t])
        for t, off in enumerate(y_offs)
    ]
    load_near = pltpu.make_async_copy(near_hbm, near, near_sem)
    for copy in load_col:
        copy.start()

    barrier = pltpu.get_barrier_semaphore()
    greeted = 0
    for off_x in range(nx):
        for off_z in range(nz):
            if off_x or off_z:
                peer = ((x + off_x) % nx * nz + (z + off_z) % nz, my_col)
                pl.semaphore_signal(barrier, inc=1, device_id=peer, device_id_type=MESH)
                greeted += 1
    for off in range(1, n_col):
        pl.semaphore_signal(barrier, inc=1, device_id=(my_row, (my_col + off) % n_col), device_id_type=MESH)
        greeted += 1
    for peer in (after_id, before_id):
        pl.semaphore_signal(barrier, inc=1, device_id=peer, device_id_type=MESH)
        greeted += 1

    load_x.wait()
    mine = table[pl.ds(leaves, leaves)].reshape(unk, LEAF)
    flipped = mine.astype(F32).T.astype(BF16)
    half = flipped.shape[0] // 2
    xt[0] = flipped
    xt[1] = jnp.concatenate([-flipped[half:], flipped[:half]], axis=0)

    load_list = pltpu.make_async_copy(list_hbm, list_ref, list_sem)
    later = [load_mid[-1], load_row, [load_list, load_near] + load_mid[0], sum(load_mid[1:-1], [])]
    a_copies = []
    for s, off_x in enumerate(x_offs):
        load_col[s].wait()
        for copy in later[s] if s < len(later) else ():
            copy.start()
        block = dot(xt[0], col[s, 0]) + dot(xt[1], col[s, 1])
        for j in range(nz):
            csend[s, j] = block[:, j * RANK : (j + 1) * RANK].astype(BF16)
        if s == 0:
            pl.semaphore_wait(barrier, greeted)
        for off_z in z_offs:
            to_z = (z + off_z) % nz
            if off_x == 0 and off_z == 0:
                arrived[s, z] = csend[s, z]
                continue
            copy = pltpu.make_async_remote_copy(
                csend.at[s, to_z],
                arrived.at[s, z],
                a_send.at[s, to_z],
                a_recv.at[s, z],
                device_id=((x + off_x) % nx * nz + to_z, my_col),
                device_id_type=MESH,
            )
            copy.start()
            a_copies.append(copy)
    for copies in later[len(x_offs) :]:
        for copy in copies:
            copy.start()

    for copy in load_mid[-1]:
        copy.wait()
    for p in range(2):
        mid_t[p] = mid[nx - 1, p].T
    for t in range(ny):
        load_row[t].wait()
        for p in range(2):
            row_t[t, p] = row[t, p].T

    tile = wy
    b_copies = []
    for s, off_x in enumerate(x_offs):
        if s == 1:
            halo = [
                pltpu.make_async_remote_copy(
                    x_hbm, table.at[pl.ds(0, leaves)], halo_send.at[0], halo_recv.at[0],
                    device_id=after_id, device_id_type=MESH,
                ),
                pltpu.make_async_remote_copy(
                    x_hbm, table.at[pl.ds(2 * leaves, leaves)], halo_send.at[1], halo_recv.at[1],
                    device_id=before_id, device_id_type=MESH,
                ),
            ]
            for copy in halo:
                copy.start()
        for off_z in z_offs:
            if off_x == 0 and off_z == 0:
                continue
            from_z = (z + nz - off_z) % nz
            slot = arrived.at[s, from_z]
            pltpu.make_async_copy(slot, slot, a_recv.at[s, from_z]).wait()
        data = jnp.concatenate([arrived[s, j] for j in range(nz)], axis=1)
        flip = swap(data)
        if s < nx - 1:
            for copy in load_mid[s]:
                copy.wait()
            part = dot_t(data, mid[s, 0]) + dot_t(flip, mid[s, 1])
            acc[...] = part if s == 0 else acc[...] + part
            continue
        for t, off_y in enumerate(y_offs):
            to_y = (y + off_y) % ny
            rows = pl.ds(t * tile, tile)
            part = acc[:, rows] + dot(data, mid_t[0, :, rows]) + dot(flip, mid_t[1, :, rows])
            for q in range(nc):
                msend[t, q] = part[:, q * RANK : (q + 1) * RANK].astype(BF16)
            for off_c in c_offs:
                to_c = (core + off_c) % nc
                if off_y == 0 and off_c == 0:
                    landed[t, core] = msend[t, core]
                    continue
                copy = pltpu.make_async_remote_copy(
                    msend.at[t, to_c],
                    landed.at[t, core],
                    b_send.at[t, to_c],
                    b_recv.at[t, core],
                    device_id=(my_row, to_y * nc + to_c),
                    device_id_type=MESH,
                )
                copy.start()
                b_copies.append(copy)

    def landing(t):
        for off_c in c_offs:
            if y_offs[t] == 0 and off_c == 0:
                continue
            from_c = (core + nc - off_c) % nc
            slot = landed.at[t, from_c]
            pltpu.make_async_copy(slot, slot, b_recv.at[t, from_c]).wait()

    def expand(t):
        data = jnp.concatenate([landed[t, q] for q in range(nc)], axis=1)
        return dot(data, row_t[t, 0]) + dot(swap(data), row_t[t, 1])

    landing(ny - 1)
    part = expand(ny - 1)
    for i in range(leaves):
        far[pl.ds(i * LEAF, LEAF), :] = part[:, i * LEAF : (i + 1) * LEAF].T
    for copy in halo:
        copy.wait_recv()
    load_near.wait()
    load_list.wait()
    for start in (0, leaves, 2 * leaves):
        side = table[pl.ds(start, leaves)].reshape(unk, LEAF)
        turned[pl.ds(start, leaves)] = turn(side).reshape(leaves, LEAF, LEAF)
    first = me * leaves - leaves
    for i in range(leaves):
        total = None
        rows = pl.ds(i * LEAF, LEAF)
        for j in range(NEAR):
            place = jnp.clip(list_ref[i, j] - first, 0, 3 * leaves - 1)
            cols = pl.ds(j * LEAF, LEAF)
            part = dot(near[0, rows, cols], table[place]) + dot(near[1, rows, cols], turned[place])
            total = part if total is None else total + part
        far[rows, :] += total

    for t in range(ny - 1):
        landing(t)
    part = sum(expand(t) for t in range(ny - 1))
    for i in range(leaves):
        rows = pl.ds(i * LEAF, LEAF)
        out_ref[rows, :] = (far[rows, :] + part[:, i * LEAF : (i + 1) * LEAF].T).astype(BF16)

    for copy in halo + a_copies + b_copies:
        copy.wait_send()


def put_out(data_ref, out_ref, sem):
    copy = pltpu.make_async_copy(data_ref, out_ref, sem)
    copy.start()
    copy.wait()


def on_device(sizes, excitation, near_list, near_blocks, col_factors, coupling, row_factors):
    nx, nz, ny, nc = sizes
    unk, cols = excitation.shape
    dma = pltpu.SemaphoreType.DMA
    hbm = pl.BlockSpec(memory_space=pl.ANY)
    rows_mid = coupling.shape[1]
    moved = sum(a.size * 2 for a in (near_blocks, col_factors, coupling, row_factors))
    response = pl.pallas_call(
        functools.partial(kernel, nx, nz, ny, nc),
        out_shape=pltpu.VMEM((unk, cols), BF16),
        in_specs=[hbm, hbm, hbm, hbm, hbm, hbm],
        out_specs=pl.BlockSpec(memory_space=pltpu.VMEM),
        scratch_shapes=[
            pltpu.SMEM(near_list.shape, jnp.int32),
            pltpu.VMEM((3 * unk // LEAF, LEAF, cols), BF16),
            pltpu.VMEM((3 * unk // LEAF, LEAF, cols), BF16),
            pltpu.VMEM(near_blocks.shape, BF16),
            pltpu.VMEM((nx, 2, unk, nz * RANK), BF16),
            pltpu.VMEM((nx, 2, rows_mid, nz * RANK), BF16),
            pltpu.VMEM((ny, 2, unk, nc * RANK), BF16),
            pltpu.VMEM((2, cols, unk), BF16),
            pltpu.VMEM((nx, nz, cols, RANK), BF16),
            pltpu.VMEM((nx, nz, cols, RANK), BF16),
            pltpu.VMEM((2, nz * RANK, rows_mid), BF16),
            pltpu.VMEM((ny, 2, nc * RANK, unk), BF16),
            pltpu.VMEM((cols, rows_mid), F32),
            pltpu.VMEM((ny, nc, cols, RANK), BF16),
            pltpu.VMEM((ny, nc, cols, RANK), BF16),
            pltpu.VMEM((unk, cols), F32),
            dma, dma, dma, dma((nx,)), dma((nx, ny)), dma((ny,)),
            dma((2,)), dma((2,)), dma((nx, nz)), dma((nx, nz)), dma((ny, nc)), dma((ny, nc)),
        ],
        compiler_params=pltpu.CompilerParams(
            collective_id=0, has_side_effects=True, vmem_limit_bytes=56 * 2**20
        ),
        cost_estimate=pl.CostEstimate(flops=128 * moved, bytes_accessed=moved, transcendentals=0),
    )(excitation.reshape(unk // LEAF, LEAF, cols), near_list, near_blocks, col_factors, coupling, row_factors)
    return response


def solution(mesh):
    nx = nz = int(round(mesh.shape["row"] ** 0.5))
    nc = 2
    ny = mesh.shape["col"] // nc
    split = P(("row", "col"), None)
    split3 = P(None, ("row", "col"), None)
    return jax.shard_map(
        functools.partial(on_device, (nx, nz, ny, nc)),
        mesh=mesh,
        in_specs=(split, split, split3, split3, split3, split3),
        out_specs=split,
        check_vma=False,
    )
```
